32 devices in a mesh: groups: 2 (over x), pair: 8 (over z, y), lam: 2 (over core).
Axes of the slice: x: 2, y: 2, z: 4, core: 2. Of those that a mesh axis runs over, the one named last changes fastest.
Arguments:
- integrals: bfloat16 [160, 1024, 1024], P(('groups', 'pair'), 'lam'), parts along dimension 0, may hold values from -6 to 6
- occ_coef: bfloat16 [1024, 32], replicated, may hold values from -0.1875 to 0.1875
- virt_coef: bfloat16 [1024, 974], replicated, may hold values from -0.1875 to 0.1875
- pair_nu: int32 [160], P('groups'), parts along dimension 0, may hold values from 0 to 1023, as said below
Outputs:
- transformed: float32 [4, 32, 32, 974], P('groups', None, 'pair', 'lam'), parts along dimension 0
The draws below stay inside these ranges and needn't reach their ends.
There are 2 independent parts, one for each index of `groups`. The reference program is written for one: setup_inputs(seed, part) draws one part's arguments, and reference() takes and returns one part's arrays. A program takes and returns all parts, laid end to end along the dimension named above; an argument that names none is the same for every part. Nothing has to cross between parts.
Inputs may be any that keep to these rules, and one draw needn't show every extreme that they name: `pair_nu`: within each block of 40 consecutive pairs the numbers are distinct, and every block holds 0 and 1023.
All inputs are finite; a program needn't handle non-finite values.
Results may differ from the reference program's by a relative error of at most 0.0029.
Values may be sent and summed in bfloat16 or wider, within the bound.
A program may use at most 64 MiB of HBM per device.

```python
import jax
import jax.numpy as jnp
from jax import lax

N = 1024
O = 32
V = 974
MUS = 2
PAIRS = 80
NUW = 40


def draw_pair_nu(key, part):
    key = jax.random.fold_in(key, 5)
    width = PAIRS // MUS
    blocks = []
    for member in range(MUS):
        first, second = jax.random.split(jax.random.fold_in(key, member))
        inner = jax.random.permutation(first, N - 2)[:width - 2].astype(jnp.int32) + 1
        ends = jnp.array([0, N - 1], dtype=jnp.int32)
        merged = jnp.concatenate([ends, inner])
        blocks.append(jax.random.permutation(second, merged).astype(jnp.int32))
    return jnp.concatenate(blocks)


def steps_of(stream_key, dims, pieces, low, largest):
    gain, own = 1.0, jax.random.fold_in(stream_key, 6)
    for dim, blocks in pieces:
        heights = jnp.exp(jax.random.uniform(jax.random.fold_in(own, dim), (blocks,), jnp.float32, low / len(pieces), largest / len(pieces)))
        gain = gain * jnp.repeat(heights, dims[dim] // blocks).reshape([-1 if axis == dim else 1 for axis in range(len(dims))])
    return gain


def bell_draw(stream_key, dims, spread, limit, pieces=(), kind=jnp.bfloat16):
    drawn = spread * jax.random.normal(stream_key, dims, jnp.float32)
    if pieces:
        drawn = drawn * steps_of(stream_key, dims, pieces, -0.22, 0.18)
    return jnp.clip(drawn, -limit, limit).astype(kind)


def setup_inputs(seed: int = 0, part: int = 0) -> dict:
    streams_of = jax.random.split(jax.random.key(seed), 5)
    part_splits = jax.random.split(jax.random.fold_in(streams_of[4], part), 5)
    return {
        "integrals": bell_draw(part_splits[0], (PAIRS, N, N), 1.0, 6.0, ((0, 8), (1, 2))),
        "occ_coef": bell_draw(streams_of[1], (N, O), N ** -0.5, 0.1875),
        "virt_coef": bell_draw(streams_of[2], (N, V), N ** -0.5, 0.1875),
        "pair_nu": draw_pair_nu(jax.random.fold_in(jax.random.fold_in(streams_of[4], part), 71), part),
    }


def reference(integrals, occ_coef, virt_coef, pair_nu):
    def one_pair(block):
        half = jnp.dot(occ_coef.T, block, preferred_element_type=jnp.float32).astype(jnp.bfloat16)
        return jnp.dot(half, virt_coef, preferred_element_type=jnp.float32)

    mo_pairs = lax.map(one_pair, integrals)
    rows = occ_coef[pair_nu].astype(jnp.float32)
    mu_ids = jnp.arange(PAIRS, dtype=jnp.int32) // NUW
    onehot = (mu_ids[:, None] == jnp.arange(MUS, dtype=jnp.int32)[None, :]).astype(jnp.float32)
    weights = onehot[:, :, None] * rows[:, None, :]
    return jnp.einsum("pmj,pia->mjia", weights, mo_pairs, precision=lax.Precision.HIGHEST)
```

```python
import functools

import jax
import jax.numpy as jnp
from jax import lax
from jax.experimental import pallas as pl
from jax.experimental.pallas import tpu as pltpu
from jax.sharding import PartitionSpec as P

MUS = 2
ROWS = 16
MESH = pl.DeviceIdType.MESH
F32 = jnp.float32
BF16 = jnp.bfloat16


def iota(shape, dim):
    return lax.broadcasted_iota(jnp.int32, shape, dim)


def selector(mask):
    return jnp.where(mask, 1.0, 0.0).astype(BF16)


def dot(a, b):
    return jnp.dot(a, b, preferred_element_type=F32)


def dot_nt(a, b):
    return lax.dot_general(a, b, (((1,), (1,)), ((), ())), preferred_element_type=F32)


def kernel(
    npair, occ, per, batches,
    integrals, occ_hbm, virt_hbm, nu_ref, out_ref,
    ints, occ_ref, virt, occ_sel, weights, own, send_a, recv_a, half_rows, mo, send_b, recv_b,
    load_sem, small_sem, send_a_sem, recv_a_sem, send_b_sem, recv_b_sem,
):
    me = lax.axis_index("pair")
    core = lax.axis_index("lam")
    half = npair // 2
    local, lam_rows, nsig = ints.shape
    own_i = occ // 2
    vcols = virt.shape[1]
    acols = vcols // 2
    wide = recv_b.shape[2]
    in_batch = ROWS // per
    feeder = me // half
    is_self = feeder == core

    load_occ = pltpu.make_async_copy(occ_hbm, occ_ref, small_sem.at[0])
    load_occ.start()
    loads = [
        pltpu.make_async_copy(integrals.at[p], ints.at[p], load_sem.at[p]) for p in range(local)
    ]
    load_virt = pltpu.make_async_copy(virt_hbm, virt, small_sem.at[1])
    for p in range(local):
        loads[p].start()
        if p == min(2, local - 1):
            load_virt.start()

    barrier = pltpu.get_barrier_semaphore()
    for j in range(1, npair):
        pl.semaphore_signal(
            barrier, inc=1,
            device_id={"pair": lax.rem(me + j, npair), "lam": feeder}, device_id_type=MESH,
        )
    pl.semaphore_signal(
        barrier, inc=1, device_id={"pair": me, "lam": 1 - core}, device_id_type=MESH
    )

    load_occ.wait()
    turned = selector(
        iota((occ, occ), 1) == ((iota((occ, occ), 0) + core * own_i) & (occ - 1))
    )
    start = pl.multiple_of(core * lam_rows, lam_rows)
    occ_sel[...] = dot_nt(turned, occ_ref[pl.ds(start, lam_rows), :]).astype(BF16)

    eye = selector(iota((occ, occ), 0) == iota((occ, occ), 1))
    occ_t = dot_nt(eye, occ_ref[...]).astype(BF16)
    pairs_all = nu_ref.shape[1]
    nbasis = occ_ref.shape[0]
    picked = selector(iota((nbasis, pairs_all), 0) == nu_ref[...])
    rows_t = dot(occ_t, picked).astype(BF16)
    mrows = MUS * occ * per
    cols = npair * ROWS
    spread = selector(
        ((iota((mrows, occ), 0) // per) & (occ - 1)) == iota((mrows, occ), 1)
    )
    tall = dot(spread, rows_t).astype(BF16)
    r = iota((mrows, cols), 0)
    c = iota((mrows, cols), 1)
    width = pairs_all // MUS
    for b in range(batches):
        cp = iota((pairs_all, cols), 1)
        place = b * in_batch + (cp & (ROWS - 1)) // per
        hit = (iota((pairs_all, cols), 0) == (cp // ROWS) * local + place) & (place < local)
        full = dot(tall, selector(hit))
        pair_of = (c // ROWS) * local + b * in_batch + (c & (ROWS - 1)) // per
        keep = ((r & (per - 1)) == (c & (per - 1))) & (
            (r >= occ * per) == (pair_of >= width)
        )
        weights[b] = jnp.where(keep, full, 0.0).astype(BF16)

    tail = local - (batches - 1) * in_batch
    if tail < in_batch:
        half_rows[batches - 1] = jnp.zeros(half_rows.shape[1:], F32)
    mo[:, vcols - vcols % 128:] = jnp.zeros((mo.shape[0], mo.shape[1] - (vcols - vcols % 128)), F32)

    pl.semaphore_wait(barrier, jnp.where(is_self, 2 * half - 1, 2 * half + 1))

    def to_sibling(p):
        return pltpu.make_async_remote_copy(
            src_ref=send_a.at[p], dst_ref=recv_a.at[p],
            send_sem=send_a_sem.at[p], recv_sem=recv_a_sem.at[p],
            device_id={"pair": me, "lam": 1 - core}, device_id_type=MESH,
        )

    def first(p):
        loads[p].wait()
        value = dot(occ_sel[...], ints[p])
        send_a[p] = value[own_i:]
        to_sibling(p).start()
        own[p] = value[:own_i]

    def to_owner(b, side, j):
        k = lax.rem(me + 1 + j, half)
        return k, pltpu.make_async_remote_copy(
            src_ref=send_b.at[b, side, pl.ds(pl.multiple_of(k * ROWS, ROWS), ROWS)],
            dst_ref=recv_b.at[b, pl.ds(pl.multiple_of(me * ROWS, ROWS), ROWS)],
            send_sem=send_b_sem.at[b, side, j], recv_sem=recv_b_sem.at[b, me],
            device_id={"pair": core * half + k, "lam": side}, device_id_type=MESH,
        )

    def second(b):
        for q in range(min(in_batch, local - b * in_batch)):
            p = b * in_batch + q
            to_sibling(p).wait_recv()
            value = own[p] + recv_a[p]
            for k in range(half):
                half_rows[b, k * ROWS + q * per:k * ROWS + (q + 1) * per, :] = (
                    value[k * per:(k + 1) * per]
                )
        if b == 0:
            load_virt.wait()
        mo[:, :vcols] = dot(half_rows[b].astype(BF16), virt[...])
        base = acols // 128 * 128
        span = min(mo.shape[1] - base, wide + 128)
        upper = mo[:, base:base + span]
        upper = pltpu.roll(upper, span - (acols - base), 1)[:, :wide]
        send_b[b, 0] = mo[:, :wide].astype(BF16)
        send_b[b, 1] = upper.astype(BF16)
        for j in range(half):
            for side in range(2):
                k, copy = to_owner(b, side, j)
                if j < half - 1:
                    copy.start()
                else:
                    mine = is_self & (core == side)

                    @pl.when(jnp.logical_not(mine))
                    def _():
                        copy.start()

                    @pl.when(mine)
                    def _():
                        rows = pl.ds(pl.multiple_of(k * ROWS, ROWS), ROWS)
                        recv_b[b, pl.ds(pl.multiple_of(me * ROWS, ROWS), ROWS), :] = (
                            send_b[b, side, rows, :]
                        )

    done = 0
    for b in range(batches):
        ready = min((b + 1) * in_batch + 1, local)
        for p in range(done, ready):
            first(p)
        done = ready
        second(b)

    for b in range(batches):
        for s in range(npair):
            landed = pltpu.make_async_remote_copy(
                src_ref=recv_b.at[b, pl.ds(s * ROWS, ROWS)],
                dst_ref=recv_b.at[b, pl.ds(s * ROWS, ROWS)],
                send_sem=send_b_sem.at[b, 0, 0], recv_sem=recv_b_sem.at[b, s],
                device_id={"pair": me, "lam": 1 - core}, device_id_type=MESH,
            )

            @pl.when(jnp.logical_not(is_self & (me == s)))
            def _():
                landed.wait_recv()
        value = dot(weights[b], recv_b[b])[:, :acols]
        if b == 0:
            out_ref[...] = value
        else:
            out_ref[...] += value

    for p in range(local):
        to_sibling(p).wait_send()
    for b in range(batches):
        for j in range(half):
            for side in range(2):
                k, copy = to_owner(b, side, j)
                if j < half - 1:
                    copy.wait_send()
                else:

                    @pl.when(jnp.logical_not(is_self & (core == side)))
                    def _():
                        copy.wait_send()


def shards(npair, integrals, occ_coef, virt_coef, pair_nu):
    local, lam_rows, nsig = integrals.shape
    nbasis, occ = occ_coef.shape
    vcols = virt_coef.shape[1]
    half = npair // 2
    per = occ // npair
    in_batch = ROWS // per
    batches = -(-local // in_batch)
    acols = vcols // 2
    wide = -(-acols // 128) * 128
    vwide = -(-vcols // 128) * 128
    own_i = occ // 2
    mrows = MUS * occ * per
    anyspace = pl.BlockSpec(memory_space=pl.ANY)
    vmem = pl.BlockSpec(memory_space=pltpu.VMEM)
    out = pl.pallas_call(
        functools.partial(kernel, npair, occ, per, batches),
        out_shape=jax.ShapeDtypeStruct((mrows, acols), F32),
        in_specs=[anyspace, anyspace, anyspace, vmem],
        out_specs=vmem,
        scratch_shapes=[
            pltpu.VMEM((local, lam_rows, nsig), BF16),
            pltpu.VMEM((nbasis, occ), BF16),
            pltpu.VMEM((nsig, vcols), BF16),
            pltpu.VMEM((occ, lam_rows), BF16),
            pltpu.VMEM((batches, mrows, npair * ROWS), BF16),
            pltpu.VMEM((local, own_i, nsig), F32),
            pltpu.VMEM((local, own_i, nsig), F32),
            pltpu.VMEM((local, own_i, nsig), F32),
            pltpu.VMEM((batches, half * ROWS, nsig), F32),
            pltpu.VMEM((half * ROWS, vwide), F32),
            pltpu.VMEM((batches, 2, half * ROWS, wide), BF16),
            pltpu.VMEM((batches, npair * ROWS, wide), BF16),
            pltpu.SemaphoreType.DMA((local,)),
            pltpu.SemaphoreType.DMA((2,)),
            pltpu.SemaphoreType.DMA((local,)),
            pltpu.SemaphoreType.DMA((local,)),
            pltpu.SemaphoreType.DMA((batches, 2, half)),
            pltpu.SemaphoreType.DMA((batches, npair)),
        ],
        compiler_params=pltpu.CompilerParams(
            collective_id=0, has_side_effects=True, vmem_limit_bytes=48 * 1024 * 1024
        ),
        name="mp2_transform",
    )(integrals, occ_coef, virt_coef, pair_nu.reshape(1, -1))
    return out.reshape(MUS, occ, per, acols)


def solution(mesh):
    in_specs = (P(("groups", "pair"), "lam", None), P(), P(), P("groups"))
    out_specs = P("groups", None, "pair", "lam")
    body = functools.partial(shards, mesh.shape["pair"])
    return jax.shard_map(body, mesh=mesh, in_specs=in_specs, out_specs=out_specs, check_vma=False)
```

```python
import functools

import jax
import jax.numpy as jnp
from jax import lax
from jax.experimental import pallas as pl
from jax.experimental.pallas import tpu as pltpu
from jax.sharding import PartitionSpec as P

MUS = 2
ROWS = 16
AHEAD = 2
WINDOW = 4
VIRT_AT = 0
MESH = pl.DeviceIdType.MESH
F32 = jnp.float32
BF16 = jnp.bfloat16


def iota(shape, dim):
    return lax.broadcasted_iota(jnp.int32, shape, dim)


def selector(mask):
    return jnp.where(mask, 1.0, 0.0).astype(BF16)


def dot(a, b):
    return jnp.dot(a, b, preferred_element_type=F32)


def dot_nt(a, b):
    return lax.dot_general(a, b, (((1,), (1,)), ((), ())), preferred_element_type=F32)


def kernel(
    npair, occ, per, batches,
    integrals, occ_hbm, virt_hbm, nu_hbm, out_ref,
    ints, occ_ref, virt, nu_ref, occ_sel, weights, own, send_a, recv_a, half_rows, mo, send_b, recv_b, send_t, recv_t,
    load_sem, small_sem, send_a_sem, recv_a_sem, send_b_sem, recv_b_sem,
):
    me = lax.axis_index("pair")
    core = lax.axis_index("lam")
    half = npair // 2
    local, lam_rows, nsig = ints.shape
    own_i = occ // 2
    vcols = virt.shape[0]
    acols = vcols // 2
    wide = recv_b.shape[2]
    in_batch = ROWS // per
    feeder = me // half
    is_self = feeder == core
    tail = local - (batches - 1) * in_batch
    fold = 2 if tail * per <= ROWS // 2 else 1
    last = batches - 1
    thin = wide // 2

    def rows_of(b):
        return ROWS // fold if b == last else ROWS

    def outgoing(b):
        return send_t if b == last and fold == 2 else send_b.at[b]

    def incoming(b):
        return recv_t if b == last and fold == 2 else recv_b.at[b]

    load_occ = pltpu.make_async_copy(occ_hbm, occ_ref, small_sem.at[0])
    load_occ.start()
    loads = [
        pltpu.make_async_copy(integrals.at[p], ints.at[p], load_sem.at[p]) for p in range(local)
    ]
    load_virt = pltpu.make_async_copy(virt_hbm, virt, small_sem.at[1])
    load_nu = pltpu.make_async_copy(nu_hbm, nu_ref, small_sem.at[2])
    for p in range(min(WINDOW, local)):
        loads[p].start()

    barrier = pltpu.get_barrier_semaphore()
    for j in range(1, npair):
        pl.semaphore_signal(
            barrier, inc=1,
            device_id={"pair": lax.rem(me + j, npair), "lam": feeder}, device_id_type=MESH,
        )
    pl.semaphore_signal(
        barrier, inc=1, device_id={"pair": me, "lam": 1 - core}, device_id_type=MESH
    )

    load_occ.wait()
    turned = selector(
        iota((occ, occ), 1) == ((iota((occ, occ), 0) + core * own_i) & (occ - 1))
    )
    start = pl.multiple_of(core * lam_rows, lam_rows)
    occ_sel[...] = dot(turned, occ_ref[:, pl.ds(start, lam_rows)]).astype(BF16)

    if tail * per < rows_of(last):
        half_rows[last] = jnp.zeros(half_rows.shape[1:], F32)
    mo[:, vcols - vcols % 128:] = jnp.zeros((mo.shape[0], mo.shape[1] - (vcols - vcols % 128)), F32)

    pl.semaphore_wait(barrier, jnp.where(is_self, 2 * half - 1, 2 * half + 1))

    def to_sibling(p):
        return pltpu.make_async_remote_copy(
            src_ref=send_a.at[p], dst_ref=recv_a.at[p],
            send_sem=send_a_sem.at[p], recv_sem=recv_a_sem.at[p],
            device_id={"pair": me, "lam": 1 - core}, device_id_type=MESH,
        )

    def first(p):
        loads[p].wait()
        if p + WINDOW < local:
            loads[p + WINDOW].start()
        if p == VIRT_AT:
            load_virt.start()
            load_nu.start()
        value = dot(occ_sel[...], ints[p])
        send_a[p] = value[own_i:]
        to_sibling(p).start()
        own[p] = value[:own_i]

    def to_owner(b, side, j):
        k = lax.rem(me + 1 + j, half)
        return k, pltpu.make_async_remote_copy(
            src_ref=outgoing(b).at[side, pl.ds(pl.multiple_of(k * ROWS, ROWS), ROWS)],
            dst_ref=incoming(b).at[pl.ds(pl.multiple_of(me * ROWS, ROWS), ROWS)],
            send_sem=send_b_sem.at[b, side, j], recv_sem=recv_b_sem.at[b, me],
            device_id={"pair": core * half + k, "lam": side}, device_id_type=MESH,
        )

    def second(b):
        size = rows_of(b)
        count = half * size
        for q in range(min(in_batch, local - b * in_batch)):
            p = b * in_batch + q
            to_sibling(p).wait_recv()
            value = own[p] + recv_a[p]
            for k in range(half):
                half_rows[b, k * size + q * per:k * size + (q + 1) * per, :] = (
                    value[k * per:(k + 1) * per]
                )
        if b == 0:
            load_virt.wait()
        mo[:count, :vcols] = dot_nt(half_rows[b, :count].astype(BF16), virt[...])
        base = acols // 128 * 128
        span = min(mo.shape[1] - base, wide + 128)
        upper = mo[:count, base:base + span]
        upper = pltpu.roll(upper, span - (acols - base), 1)[:, :wide]
        for side, value in enumerate((mo[:count, :wide], upper)):
            if size < ROWS:
                value = jnp.concatenate(
                    [
                        value[k * size:(k + 1) * size, h * thin:(h + 1) * thin]
                        for k in range(half) for h in range(2)
                    ],
                    axis=0,
                )
            outgoing(b)[side] = value.astype(BF16)
        for j in range(half):
            for side in range(2):
                k, copy = to_owner(b, side, j)
                if j < half - 1:
                    copy.start()
                else:
                    mine = is_self & (core == side)

                    @pl.when(jnp.logical_not(mine))
                    def _():
                        copy.start()

                    @pl.when(mine)
                    def _():
                        rows = pl.ds(pl.multiple_of(k * ROWS, ROWS), ROWS)
                        incoming(b)[pl.ds(pl.multiple_of(me * ROWS, ROWS), ROWS), :] = (
                            outgoing(b)[side, rows, :]
                        )

    done = 0
    for b in range(batches):
        ready = min((b + 1) * in_batch + AHEAD, local)
        for p in range(done, ready):
            first(p)
        done = ready
        second(b)

    load_nu.wait()
    pairs_all = nu_ref.shape[1]
    nbasis = occ_ref.shape[1]
    picked = selector(iota((nbasis, pairs_all), 0) == nu_ref[...])
    rows_t = dot(occ_ref[...], picked).astype(BF16)
    mrows = MUS * occ * per
    cols = npair * ROWS
    spread = selector(
        ((iota((mrows, occ), 0) // per) & (occ - 1)) == iota((mrows, occ), 1)
    )
    tall = dot(spread, rows_t).astype(BF16)
    r = iota((mrows, cols), 0)
    c = iota((mrows, cols), 1)
    width = pairs_all // MUS
    for n in range(batches + fold - 1):
        b = min(n, last)
        size = rows_of(b)
        cp = iota((pairs_all, cols), 1)
        place = b * in_batch + (cp & (size - 1)) // per
        hit = (iota((pairs_all, cols), 0) == (cp // ROWS) * local + place) & (place < local)
        if size < ROWS:
            hit = hit & ((cp & (ROWS - 1)) // size == n - b)
        full = dot(tall, selector(hit))
        pair_of = (c // ROWS) * local + b * in_batch + (c & (size - 1)) // per
        keep = ((r & (per - 1)) == (c & (per - 1))) & (
            (r >= occ * per) == (pair_of >= width)
        )
        weights[n] = jnp.where(keep, full, 0.0).astype(BF16)

    for b in range(batches):
        for s in range(npair):
            landed = pltpu.make_async_remote_copy(
                src_ref=incoming(b).at[pl.ds(s * ROWS, ROWS)],
                dst_ref=incoming(b).at[pl.ds(s * ROWS, ROWS)],
                send_sem=send_b_sem.at[b, 0, 0], recv_sem=recv_b_sem.at[b, s],
                device_id={"pair": me, "lam": 1 - core}, device_id_type=MESH,
            )

            @pl.when(jnp.logical_not(is_self & (me == s)))
            def _():
                landed.wait_recv()
        if rows_of(b) < ROWS:
            value = jnp.concatenate([dot(weights[b + h], recv_t[...]) for h in range(2)], axis=1)
        else:
            value = dot(weights[b], recv_b[b])
        if b == 0:
            out_ref[...] = value[:, :acols]
        else:
            out_ref[...] += value[:, :acols]

    for p in range(local):
        to_sibling(p).wait_send()
    for b in range(batches):
        for j in range(half):
            for side in range(2):
                k, copy = to_owner(b, side, j)
                if j < half - 1:
                    copy.wait_send()
                else:

                    @pl.when(jnp.logical_not(is_self & (core == side)))
                    def _():
                        copy.wait_send()


def shards(npair, integrals, occ_coef, virt_coef, pair_nu):
    local, lam_rows, nsig = integrals.shape
    nbasis = occ_coef.shape[0]
    occ = occ_coef.shape[1]
    vcols = virt_coef.shape[1]
    half = npair // 2
    per = occ // npair
    in_batch = ROWS // per
    batches = -(-local // in_batch)
    acols = vcols // 2
    wide = -(-acols // 128) * 128
    vwide = -(-vcols // 128) * 128
    own_i = occ // 2
    mrows = MUS * occ * per
    pairs_all = pair_nu.shape[0]
    hbm = pl.BlockSpec(memory_space=pltpu.HBM)
    vmem = pl.BlockSpec(memory_space=pltpu.VMEM)
    out = pl.pallas_call(
        functools.partial(kernel, npair, occ, per, batches),
        out_shape=jax.ShapeDtypeStruct((mrows, acols), F32),
        in_specs=[hbm, hbm, hbm, hbm],
        out_specs=vmem,
        scratch_shapes=[
            pltpu.VMEM((local, lam_rows, nsig), BF16),
            pltpu.VMEM((occ, nbasis), BF16),
            pltpu.VMEM((vcols, nsig), BF16),
            pltpu.VMEM((1, pairs_all), jnp.int32),
            pltpu.VMEM((occ, lam_rows), BF16),
            pltpu.VMEM((batches + 1, mrows, npair * ROWS), BF16),
            pltpu.VMEM((local, own_i, nsig), F32),
            pltpu.VMEM((local, own_i, nsig), F32),
            pltpu.VMEM((local, own_i, nsig), F32),
            pltpu.VMEM((batches, half * ROWS, nsig), F32),
            pltpu.VMEM((half * ROWS, vwide), F32),
            pltpu.VMEM((batches, 2, half * ROWS, wide), BF16),
            pltpu.VMEM((batches, npair * ROWS, wide), BF16),
            pltpu.VMEM((2, half * ROWS, wide // 2), BF16),
            pltpu.VMEM((npair * ROWS, wide // 2), BF16),
            pltpu.SemaphoreType.DMA((local,)),
            pltpu.SemaphoreType.DMA((3,)),
            pltpu.SemaphoreType.DMA((local,)),
            pltpu.SemaphoreType.DMA((local,)),
            pltpu.SemaphoreType.DMA((batches, 2, half)),
            pltpu.SemaphoreType.DMA((batches, npair)),
        ],
        compiler_params=pltpu.CompilerParams(
            collective_id=0, has_side_effects=True, vmem_limit_bytes=64 * 1024 * 1024
        ),
        name="mp2_transform",
    )(integrals, occ_coef.T, virt_coef.T, pair_nu.reshape(1, -1))
    return out.reshape(MUS, occ, per, acols)


def solution(mesh):
    in_specs = (P(("groups", "pair"), "lam", None), P(), P(), P("groups"))
    out_specs = P("groups", None, "pair", "lam")
    body = functools.partial(shards, mesh.shape["pair"])
    return jax.shard_map(body, mesh=mesh, in_specs=in_specs, out_specs=out_specs, check_vma=False)
```

```python
import functools

import jax
import jax.numpy as jnp
from jax import lax
from jax.experimental import pallas as pl
from jax.experimental.pallas import tpu as pltpu
from jax.sharding import PartitionSpec as P

MUS = 2
ROWS = 16
AHEAD = 0
LIMIT = 64 * 1024 * 1024
WINDOW = 5
VIRT_AT = 1
MESH = pl.DeviceIdType.MESH
F32 = jnp.float32
BF16 = jnp.bfloat16


def iota(shape, dim):
    return lax.broadcasted_iota(jnp.int32, shape, dim)


def selector(mask):
    return jnp.where(mask, 1.0, 0.0).astype(BF16)


def dot(a, b):
    return jnp.dot(a, b, preferred_element_type=F32)


def dot_nt(a, b):
    return lax.dot_general(a, b, (((1,), (1,)), ((), ())), preferred_element_type=F32)


def kernel(
    npair, occ, per, batches,
    integrals, occ_hbm, virt_hbm, nu_hbm, recv_b, recv_t, weights_out,
    ints, occ_ref, virt, nu_ref, occ_sel, weights, own, send_a, recv_a, half_rows, mo, send_b, send_t,
    load_sem, small_sem, send_a_sem, recv_a_sem, send_b_sem, recv_b_sem, own_sem,
):
    me = lax.axis_index("pair")
    core = lax.axis_index("lam")
    half = npair // 2
    local, lam_rows, nsig = ints.shape
    own_i = occ // 2
    vcols = virt.shape[0]
    acols = vcols // 2
    wide = send_b.shape[3]
    in_batch = ROWS // per
    feeder = me // half
    is_self = feeder == core
    tail = local - (batches - 1) * in_batch
    fold = 2 if tail * per <= ROWS // 2 else 1
    last = batches - 1
    thin = wide // 2

    def rows_of(b):
        return ROWS // fold if b == last else ROWS

    def outgoing(b):
        return send_t if b == last and fold == 2 else send_b.at[b]

    def incoming(b):
        return recv_t if b == last and fold == 2 else recv_b.at[b]

    load_occ = pltpu.make_async_copy(occ_hbm, occ_ref, small_sem.at[0])
    load_occ.start()
    loads = [
        pltpu.make_async_copy(integrals.at[p], ints.at[p], load_sem.at[p]) for p in range(local)
    ]
    load_virt = pltpu.make_async_copy(virt_hbm, virt, small_sem.at[1])
    load_nu = pltpu.make_async_copy(nu_hbm, nu_ref, small_sem.at[2])
    for p in range(min(WINDOW, local)):
        loads[p].start()

    barrier = pltpu.get_barrier_semaphore()
    for j in range(1, npair):
        pl.semaphore_signal(
            barrier, inc=1,
            device_id={"pair": lax.rem(me + j, npair), "lam": feeder}, device_id_type=MESH,
        )
    pl.semaphore_signal(
        barrier, inc=1, device_id={"pair": me, "lam": 1 - core}, device_id_type=MESH
    )

    load_occ.wait()
    turned = selector(
        iota((occ, occ), 1) == ((iota((occ, occ), 0) + core * own_i) & (occ - 1))
    )
    start = pl.multiple_of(core * lam_rows, lam_rows)
    occ_sel[...] = dot(turned, occ_ref[:, pl.ds(start, lam_rows)]).astype(BF16)

    if tail * per < rows_of(last):
        half_rows[last] = jnp.zeros(half_rows.shape[1:], F32)
    mo[:, vcols - vcols % 128:] = jnp.zeros((mo.shape[0], mo.shape[1] - (vcols - vcols % 128)), F32)

    pl.semaphore_wait(barrier, jnp.where(is_self, 2 * half - 1, 2 * half + 1))

    def to_sibling(p):
        return pltpu.make_async_remote_copy(
            src_ref=send_a.at[p], dst_ref=recv_a.at[p],
            send_sem=send_a_sem.at[p], recv_sem=recv_a_sem.at[p],
            device_id={"pair": me, "lam": 1 - core}, device_id_type=MESH,
        )

    def first(p):
        loads[p].wait()
        if p + WINDOW < local:
            loads[p + WINDOW].start()
        if p == VIRT_AT:
            load_virt.start()
            load_nu.start()
        value = dot(occ_sel[...], ints[p])
        send_a[p] = value[own_i:]
        to_sibling(p).start()
        own[p] = value[:own_i]

    def to_owner(b, side, j):
        k = lax.rem(me + 1 + j, half)
        return k, pltpu.make_async_remote_copy(
            src_ref=outgoing(b).at[side, pl.ds(pl.multiple_of(k * ROWS, ROWS), ROWS)],
            dst_ref=incoming(b).at[pl.ds(pl.multiple_of(me * ROWS, ROWS), ROWS)],
            send_sem=send_b_sem.at[b, side, j], recv_sem=recv_b_sem.at[b, me],
            device_id={"pair": core * half + k, "lam": side}, device_id_type=MESH,
        )

    def keep_own(b, side, k):
        return pltpu.make_async_copy(
            outgoing(b).at[side, pl.ds(pl.multiple_of(k * ROWS, ROWS), ROWS)],
            incoming(b).at[pl.ds(pl.multiple_of(me * ROWS, ROWS), ROWS)],
            own_sem.at[b, side],
        )

    def second(b):
        size = rows_of(b)
        count = half * size
        for q in range(min(in_batch, local - b * in_batch)):
            p = b * in_batch + q
            to_sibling(p).wait_recv()
            value = own[p] + recv_a[p]
            for k in range(half):
                half_rows[b, k * size + q * per:k * size + (q + 1) * per, :] = (
                    value[k * per:(k + 1) * per]
                )
        if b == 0:
            load_virt.wait()
        mo[:count, :vcols] = dot_nt(half_rows[b, :count].astype(BF16), virt[...])
        base = acols // 128 * 128
        span = min(mo.shape[1] - base, wide + 128)
        upper = mo[:count, base:base + span]
        upper = pltpu.roll(upper, span - (acols - base), 1)[:, :wide]
        for side, value in enumerate((mo[:count, :wide], upper)):
            if size < ROWS:
                value = jnp.concatenate(
                    [
                        value[k * size:(k + 1) * size, h * thin:(h + 1) * thin]
                        for k in range(half) for h in range(2)
                    ],
                    axis=0,
                )
            outgoing(b)[side] = value.astype(BF16)
        for j in range(half):
            for side in range(2):
                k, copy = to_owner(b, side, j)
                if j < half - 1:
                    copy.start()
                else:
                    mine = is_self & (core == side)

                    @pl.when(jnp.logical_not(mine))
                    def _():
                        copy.start()

                    @pl.when(mine)
                    def _():
                        keep_own(b, side, k).start()

    done = 0
    for b in range(batches):
        ready = min((b + 1) * in_batch + AHEAD, local)
        for p in range(done, ready):
            first(p)
        done = ready
        second(b)

    load_nu.wait()
    pairs_all = nu_ref.shape[1]
    nbasis = occ_ref.shape[1]
    picked = selector(iota((nbasis, pairs_all), 0) == nu_ref[...])
    rows_t = dot(occ_ref[...], picked).astype(BF16)
    mrows = MUS * occ * per
    cols = npair * ROWS
    spread = selector(
        ((iota((mrows, occ), 0) // per) & (occ - 1)) == iota((mrows, occ), 1)
    )
    tall = dot(spread, rows_t).astype(BF16)
    r = iota((mrows, cols), 0)
    c = iota((mrows, cols), 1)
    width = pairs_all // MUS
    for n in range(batches + fold - 1):
        b = min(n, last)
        size = rows_of(b)
        cp = iota((pairs_all, cols), 1)
        place = b * in_batch + (cp & (size - 1)) // per
        hit = (iota((pairs_all, cols), 0) == (cp // ROWS) * local + place) & (place < local)
        if size < ROWS:
            hit = hit & ((cp & (ROWS - 1)) // size == n - b)
        full = dot(tall, selector(hit))
        pair_of = (c // ROWS) * local + b * in_batch + (c & (size - 1)) // per
        keep = ((r & (per - 1)) == (c & (per - 1))) & (
            (r >= occ * per) == (pair_of >= width)
        )
        weights[n] = jnp.where(keep, full, 0.0).astype(BF16)

    save = pltpu.make_async_copy(weights, weights_out, small_sem.at[0])
    save.start()
    for b in range(batches):
        for s in range(npair):
            landed = pltpu.make_async_remote_copy(
                src_ref=incoming(b).at[pl.ds(s * ROWS, ROWS)],
                dst_ref=incoming(b).at[pl.ds(s * ROWS, ROWS)],
                send_sem=send_b_sem.at[b, 0, 0], recv_sem=recv_b_sem.at[b, s],
                device_id={"pair": me, "lam": 1 - core}, device_id_type=MESH,
            )

            @pl.when(jnp.logical_not(is_self & (me == s)))
            def _():
                landed.wait_recv()
    save.wait()
    for p in range(local):
        to_sibling(p).wait_send()
    for b in range(batches):
        for j in range(half):
            for side in range(2):
                k, copy = to_owner(b, side, j)
                if j < half - 1:
                    copy.wait_send()
                else:

                    mine = is_self & (core == side)

                    @pl.when(jnp.logical_not(mine))
                    def _():
                        copy.wait_send()

                    @pl.when(mine)
                    def _():
                        keep_own(b, side, k).wait()


def finish(recv_b, recv_t, weights, out_ref):
    batches = recv_b.shape[0]
    acols = out_ref.shape[-1]
    total = None
    full = batches - (weights.shape[0] - batches)
    for b in range(full):
        value = dot(weights[b], recv_b[b])
        total = value if total is None else total + value
    if full < batches:
        value = jnp.concatenate([dot(weights[full + h], recv_t[...]) for h in range(2)], axis=1)
        total = value if total is None else total + value
    out_ref[...] = total[:, :acols].reshape(out_ref.shape)


def shards(npair, integrals, occ_coef, virt_coef, pair_nu):
    local, lam_rows, nsig = integrals.shape
    nbasis = occ_coef.shape[0]
    occ = occ_coef.shape[1]
    vcols = virt_coef.shape[1]
    half = npair // 2
    per = occ // npair
    in_batch = ROWS // per
    batches = -(-local // in_batch)
    acols = vcols // 2
    wide = -(-acols // 128) * 128
    vwide = -(-vcols // 128) * 128
    own_i = occ // 2
    mrows = MUS * occ * per
    pairs_all = pair_nu.shape[0]
    tail = local - (batches - 1) * in_batch
    terms = batches + (1 if tail * per <= ROWS // 2 else 0)
    anyspace = pl.BlockSpec(memory_space=pl.ANY)
    hbm = pl.BlockSpec(memory_space=pltpu.HBM)
    vmem = pl.BlockSpec(memory_space=pltpu.VMEM)
    recv_b, recv_t, weights = pl.pallas_call(
        functools.partial(kernel, npair, occ, per, batches),
        out_shape=(
            jax.ShapeDtypeStruct((batches, npair * ROWS, wide), BF16),
            jax.ShapeDtypeStruct((npair * ROWS, wide // 2), BF16),
            jax.ShapeDtypeStruct((terms, mrows, npair * ROWS), BF16),
        ),
        in_specs=[hbm, hbm, hbm, hbm],
        out_specs=(anyspace, anyspace, anyspace),
        scratch_shapes=[
            pltpu.VMEM((local, lam_rows, nsig), BF16),
            pltpu.VMEM((occ, nbasis), BF16),
            pltpu.VMEM((vcols, nsig), BF16),
            pltpu.VMEM((1, pairs_all), jnp.int32),
            pltpu.VMEM((occ, lam_rows), BF16),
            pltpu.VMEM((terms, mrows, npair * ROWS), BF16),
            pltpu.VMEM((local, own_i, nsig), F32),
            pltpu.VMEM((local, own_i, nsig), F32),
            pltpu.VMEM((local, own_i, nsig), F32),
            pltpu.VMEM((batches, half * ROWS, nsig), F32),
            pltpu.VMEM((half * ROWS, vwide), F32),
            pltpu.VMEM((batches, 2, half * ROWS, wide), BF16),
            pltpu.VMEM((2, half * ROWS, wide // 2), BF16),
            pltpu.SemaphoreType.DMA((local,)),
            pltpu.SemaphoreType.DMA((3,)),
            pltpu.SemaphoreType.DMA((local,)),
            pltpu.SemaphoreType.DMA((local,)),
            pltpu.SemaphoreType.DMA((batches, 2, half)),
            pltpu.SemaphoreType.DMA((batches, npair)),
            pltpu.SemaphoreType.DMA((batches, 2)),
        ],
        compiler_params=pltpu.CompilerParams(
            collective_id=0, has_side_effects=True, vmem_limit_bytes=LIMIT
        ),
        name="mp2_transform",
    )(integrals, occ_coef.T, virt_coef.T, pair_nu.reshape(1, -1))
    return pl.pallas_call(
        finish,
        out_shape=jax.ShapeDtypeStruct((MUS, occ, per, acols), F32),
        in_specs=[vmem, vmem, vmem],
        out_specs=vmem,
        compiler_params=pltpu.CompilerParams(vmem_limit_bytes=LIMIT),
        name="pair_contraction",
    )(recv_b, recv_t, weights)


def solution(mesh):
    in_specs = (P(("groups", "pair"), "lam", None), P(), P(), P("groups"))
    out_specs = P("groups", None, "pair", "lam")
    body = functools.partial(shards, mesh.shape["pair"])
    return jax.shard_map(body, mesh=mesh, in_specs=in_specs, out_specs=out_specs, check_vma=False)
```

```python
import functools

import jax
import jax.numpy as jnp
from jax import lax
from jax.experimental import pallas as pl
from jax.experimental.pallas import tpu as pltpu
from jax.sharding import PartitionSpec as P

MUS = 2
ROWS = 16
AHEAD = 0
LIMIT = 64 * 1024 * 1024
WINDOW = 5
VIRT_AT = 1
MESH = pl.DeviceIdType.MESH
F32 = jnp.float32
BF16 = jnp.bfloat16


def iota(shape, dim):
    return lax.broadcasted_iota(jnp.int32, shape, dim)


def selector(mask):
    return jnp.where(mask, 1.0, 0.0).astype(BF16)


def dot(a, b):
    return jnp.dot(a, b, preferred_element_type=F32)


def dot_nt(a, b):
    return lax.dot_general(a, b, (((1,), (1,)), ((), ())), preferred_element_type=F32)


def kernel(
    npair, occ, per, batches,
    integrals, occ_hbm, virt_hbm, nu_hbm, recv_b, recv_t, weights_out,
    ints, occ_ref, virt, nu_ref, occ_sel, weights, own, send_a, recv_a, half_rows, mo, send_b, send_t,
    load_sem, small_sem, send_a_sem, recv_a_sem, send_b_sem, recv_b_sem, own_sem,
):
    me = lax.axis_index("pair")
    core = lax.axis_index("lam")
    half = npair // 2
    local, lam_rows, nsig = ints.shape
    own_i = occ // 2
    vcols = virt.shape[0]
    acols = vcols // 2
    wide = send_b.shape[3]
    in_batch = ROWS // per
    feeder = me // half
    is_self = feeder == core
    tail = local - (batches - 1) * in_batch
    fold = 2 if tail * per <= ROWS // 2 else 1
    last = batches - 1
    thin = wide // 2

    def rows_of(b):
        return ROWS // fold if b == last else ROWS

    def outgoing(b):
        return send_t if b == last and fold == 2 else send_b.at[b]

    def incoming(b):
        return recv_t if b == last and fold == 2 else recv_b.at[b]

    load_occ = pltpu.make_async_copy(occ_hbm, occ_ref, small_sem.at[0])
    load_occ.start()
    loads = [
        pltpu.make_async_copy(integrals.at[p], ints.at[p], load_sem.at[p]) for p in range(local)
    ]
    load_virt = pltpu.make_async_copy(virt_hbm, virt, small_sem.at[1])
    load_nu = pltpu.make_async_copy(nu_hbm, nu_ref, small_sem.at[2])
    for p in range(min(WINDOW, local)):
        loads[p].start()

    barrier = pltpu.get_barrier_semaphore()
    for j in range(1, npair):
        pl.semaphore_signal(
            barrier, inc=1,
            device_id={"pair": lax.rem(me + j, npair), "lam": feeder}, device_id_type=MESH,
        )
    pl.semaphore_signal(
        barrier, inc=1, device_id={"pair": me, "lam": 1 - core}, device_id_type=MESH
    )

    load_occ.wait()
    turned = selector(
        iota((occ, occ), 1) == ((iota((occ, occ), 0) + core * own_i) & (occ - 1))
    )
    start = pl.multiple_of(core * lam_rows, lam_rows)
    occ_sel[...] = dot(turned, occ_ref[:, pl.ds(start, lam_rows)]).astype(BF16)

    if tail * per < rows_of(last):
        half_rows[last] = jnp.zeros(half_rows.shape[1:], F32)
    mo[:, vcols - vcols % 128:] = jnp.zeros((mo.shape[0], mo.shape[1] - (vcols - vcols % 128)), F32)

    pl.semaphore_wait(barrier, jnp.where(is_self, 2 * half - 1, 2 * half + 1))

    def to_sibling(p):
        return pltpu.make_async_remote_copy(
            src_ref=send_a.at[p], dst_ref=recv_a.at[p],
            send_sem=send_a_sem.at[p], recv_sem=recv_a_sem.at[p],
            device_id={"pair": me, "lam": 1 - core}, device_id_type=MESH,
        )

    def first(p):
        loads[p].wait()
        if p + WINDOW < local:
            loads[p + WINDOW].start()
        if p == VIRT_AT:
            load_virt.start()
            load_nu.start()
        value = dot(occ_sel[...], ints[p])
        send_a[p] = value[own_i:]
        to_sibling(p).start()
        own[p] = value[:own_i]

    def to_owner(b, side, j):
        k = lax.rem(me + 1 + j, half)
        return k, pltpu.make_async_remote_copy(
            src_ref=outgoing(b).at[side, pl.ds(pl.multiple_of(k * ROWS, ROWS), ROWS)],
            dst_ref=incoming(b).at[pl.ds(pl.multiple_of(me * ROWS, ROWS), ROWS)],
            send_sem=send_b_sem.at[b, side, j], recv_sem=recv_b_sem.at[b, me],
            device_id={"pair": core * half + k, "lam": side}, device_id_type=MESH,
        )

    def keep_own(b, side, k):
        return pltpu.make_async_copy(
            outgoing(b).at[side, pl.ds(pl.multiple_of(k * ROWS, ROWS), ROWS)],
            incoming(b).at[pl.ds(pl.multiple_of(me * ROWS, ROWS), ROWS)],
            own_sem.at[b, side],
        )

    def second(b):
        size = rows_of(b)
        count = half * size
        for q in range(min(in_batch, local - b * in_batch)):
            p = b * in_batch + q
            to_sibling(p).wait_recv()
            value = own[p] + recv_a[p]
            for k in range(half):
                half_rows[b, k * size + q * per:k * size + (q + 1) * per, :] = (
                    value[k * per:(k + 1) * per]
                )
        if b == 0:
            load_virt.wait()
        mo[:count, :vcols] = dot_nt(half_rows[b, :count].astype(BF16), virt[...])
        base = acols // 128 * 128
        span = min(mo.shape[1] - base, wide + 128)
        upper = mo[:count, base:base + span]
        upper = pltpu.roll(upper, span - (acols - base), 1)[:, :wide]
        for side, value in enumerate((mo[:count, :wide], upper)):
            if size < ROWS:
                value = jnp.concatenate(
                    [
                        value[k * size:(k + 1) * size, h * thin:(h + 1) * thin]
                        for k in range(half) for h in range(2)
                    ],
                    axis=0,
                )
            outgoing(b)[side] = value.astype(BF16)
        for j in range(half):
            for side in range(2):
                k, copy = to_owner(b, side, j)
                if j < half - 1:
                    copy.start()
                else:
                    mine = is_self & (core == side)

                    @pl.when(jnp.logical_not(mine))
                    def _():
                        copy.start()

                    @pl.when(mine)
                    def _():
                        keep_own(b, side, k).start()

    done = 0
    for b in range(batches):
        ready = min((b + 1) * in_batch + AHEAD, local)
        for p in range(done, ready):
            first(p)
        done = ready
        second(b)

    load_nu.wait()
    pairs_all = nu_ref.shape[1]
    nbasis = occ_ref.shape[1]
    picked = selector(iota((nbasis, pairs_all), 0) == nu_ref[...])
    rows_t = dot(occ_ref[...], picked).astype(BF16)
    mrows = MUS * occ * per
    cols = npair * ROWS
    spread = selector(
        ((iota((mrows, occ), 0) // per) & (occ - 1)) == iota((mrows, occ), 1)
    )
    tall = dot(spread, rows_t).astype(BF16)
    r = iota((mrows, cols), 0)
    c = iota((mrows, cols), 1)
    width = pairs_all // MUS
    for n in range(batches + fold - 1):
        b = min(n, last)
        size = rows_of(b)
        cp = iota((pairs_all, cols), 1)
        place = b * in_batch + (cp & (size - 1)) // per
        hit = (iota((pairs_all, cols), 0) == (cp // ROWS) * local + place) & (place < local)
        if size < ROWS:
            hit = hit & ((cp & (ROWS - 1)) // size == n - b)
        full = dot(tall, selector(hit))
        pair_of = (c // ROWS) * local + b * in_batch + (c & (size - 1)) // per
        keep = ((r & (per - 1)) == (c & (per - 1))) & (
            (r >= occ * per) == (pair_of >= width)
        )
        weights[n] = jnp.where(keep, full, 0.0).astype(BF16)

    save = pltpu.make_async_copy(weights, weights_out, small_sem.at[0])
    save.start()
    for b in range(batches):
        for s in range(npair):
            landed = pltpu.make_async_remote_copy(
                src_ref=incoming(b).at[pl.ds(s * ROWS, ROWS)],
                dst_ref=incoming(b).at[pl.ds(s * ROWS, ROWS)],
                send_sem=send_b_sem.at[b, 0, 0], recv_sem=recv_b_sem.at[b, s],
                device_id={"pair": me, "lam": 1 - core}, device_id_type=MESH,
            )

            @pl.when(jnp.logical_not(is_self & (me == s)))
            def _():
                landed.wait_recv()
    save.wait()
    for p in range(local):
        to_sibling(p).wait_send()
    for b in range(batches):
        for j in range(half):
            for side in range(2):
                k, copy = to_owner(b, side, j)
                if j < half - 1:
                    copy.wait_send()
                else:

                    mine = is_self & (core == side)

                    @pl.when(jnp.logical_not(mine))
                    def _():
                        copy.wait_send()

                    @pl.when(mine)
                    def _():
                        keep_own(b, side, k).wait()


def finish(full, folded, recv_b, recv_t, weights, out_ref):
    acols = out_ref.shape[-1]
    total = None
    for b in range(full):
        value = dot(weights[b], recv_b[b])
        total = value if total is None else total + value
    if folded:
        value = jnp.concatenate([dot(weights[full + h], recv_t[...]) for h in range(2)], axis=1)
        total = value if total is None else total + value
    out_ref[...] = total[:, :acols].reshape(out_ref.shape)


def shards(npair, integrals, occ_coef, virt_coef, pair_nu):
    local, lam_rows, nsig = integrals.shape
    nbasis = occ_coef.shape[0]
    occ = occ_coef.shape[1]
    vcols = virt_coef.shape[1]
    half = npair // 2
    per = occ // npair
    in_batch = ROWS // per
    batches = -(-local // in_batch)
    acols = vcols // 2
    wide = -(-acols // 128) * 128
    vwide = -(-vcols // 128) * 128
    own_i = occ // 2
    mrows = MUS * occ * per
    pairs_all = pair_nu.shape[0]
    tail = local - (batches - 1) * in_batch
    terms = batches + (1 if tail * per <= ROWS // 2 else 0)
    anyspace = pl.BlockSpec(memory_space=pl.ANY)
    hbm = pl.BlockSpec(memory_space=pltpu.HBM)
    vmem = pl.BlockSpec(memory_space=pltpu.VMEM)
    recv_b, recv_t, weights = pl.pallas_call(
        functools.partial(kernel, npair, occ, per, batches),
        out_shape=(
            jax.ShapeDtypeStruct((max(2 * batches - terms, 1), npair * ROWS, wide), BF16),
            jax.ShapeDtypeStruct((npair * ROWS, wide // 2), BF16),
            jax.ShapeDtypeStruct((terms, mrows, npair * ROWS), BF16),
        ),
        in_specs=[hbm, hbm, hbm, hbm],
        out_specs=(anyspace, anyspace, anyspace),
        scratch_shapes=[
            pltpu.VMEM((local, lam_rows, nsig), BF16),
            pltpu.VMEM((occ, nbasis), BF16),
            pltpu.VMEM((vcols, nsig), BF16),
            pltpu.VMEM((1, pairs_all), jnp.int32),
            pltpu.VMEM((occ, lam_rows), BF16),
            pltpu.VMEM((terms, mrows, npair * ROWS), BF16),
            pltpu.VMEM((local, own_i, nsig), F32),
            pltpu.VMEM((local, own_i, nsig), F32),
            pltpu.VMEM((local, own_i, nsig), F32),
            pltpu.VMEM((batches, half * ROWS, nsig), F32),
            pltpu.VMEM((half * ROWS, vwide), F32),
            pltpu.VMEM((batches, 2, half * ROWS, wide), BF16),
            pltpu.VMEM((2, half * ROWS, wide // 2), BF16),
            pltpu.SemaphoreType.DMA((local,)),
            pltpu.SemaphoreType.DMA((3,)),
            pltpu.SemaphoreType.DMA((local,)),
            pltpu.SemaphoreType.DMA((local,)),
            pltpu.SemaphoreType.DMA((batches, 2, half)),
            pltpu.SemaphoreType.DMA((batches, npair)),
            pltpu.SemaphoreType.DMA((batches, 2)),
        ],
        compiler_params=pltpu.CompilerParams(
            collective_id=0, has_side_effects=True, vmem_limit_bytes=LIMIT
        ),
        name="mp2_transform",
    )(integrals, occ_coef.T, virt_coef.T, pair_nu.reshape(1, -1))
    return pl.pallas_call(
        functools.partial(finish, 2 * batches - terms, terms > batches),
        out_shape=jax.ShapeDtypeStruct((MUS, occ, per, acols), F32),
        in_specs=[vmem, vmem, vmem],
        out_specs=vmem,
        compiler_params=pltpu.CompilerParams(vmem_limit_bytes=LIMIT),
        name="pair_contraction",
    )(recv_b, recv_t, weights)


def solution(mesh):
    in_specs = (P(("groups", "pair"), "lam", None), P(), P(), P("groups"))
    out_specs = P("groups", None, "pair", "lam")
    body = functools.partial(shards, mesh.shape["pair"])
    return jax.shard_map(body, mesh=mesh, in_specs=in_specs, out_specs=out_specs, check_vma=False)
```
